512 devices in a mesh: group: 8 (over x, z_hi), dev: 64 (over y, z_lo, core).
Axes of the slice: x: 4, y: 8, z: 8 (z_hi: 2, z_lo: 4; z = z_hi * 4 + z_lo), core: 2. Of those that a mesh axis runs over, the one named last changes fastest.
Arguments:
- tokens: bfloat16 [8192, 8192], P(('group', 'dev'))
- query_grad: bfloat16 [8192, 8192], P(('group', 'dev')), may hold values from -0.06591797 to 0.06591797
- gain: float32 [8192], replicated, may hold values from 0.1 to 1.9
- master: float32 [64, 8, 8, 16384], P('dev', 'group'), may hold values from -6 to 6
- momentum: float32 [64, 8, 8, 16384], P('dev', 'group'), may hold values from -6 to 6
- owner: int32 [64, 64], replicated, may hold values from 0 to 7, as said below
Outputs:
- master_new: float32 [64, 8, 8, 16384], P('dev', 'group')
- momentum_new: float32 [64, 8, 8, 16384], P('dev', 'group')
- params_new: bfloat16 [8192, 8192], P(None, 'dev')
The draws below stay inside these ranges and needn't reach their ends.
Inputs may be any that keep to these rules, and one draw needn't show every extreme that they name: `owner`: for every column block d, each group owns exactly 8 of its 64 partitions.
All inputs are finite; a program needn't handle non-finite values.
Results may differ from the reference program's by a relative error of at most 0.013.
Values may be sent and summed in bfloat16 or wider, within the bound.
No kernel may reach another device: no remote copies, remote signals or barrier semaphores. Data moves between devices by JAX's collectives and lax.ppermute only.
A program may use at most 128 MiB of HBM per device.

```python
import math
import jax
import jax.numpy as jnp
from jax import lax

D = 8192
PART = 16384
COLS = 128
TOKENS = 8192
K = 64
KG = 8
N_GROUP = 8
N_DEV = 64


def draw_tokens(key, part):
    key = jax.random.fold_in(key, 11)
    key_base, key_rows, key_cols = jax.random.split(key, 3)
    noise = jnp.clip(jax.random.normal(key_base, (TOKENS, D), jnp.float32), -5.0, 5.0)
    row_scale = jnp.exp(jax.random.uniform(key_rows, (TOKENS, 1), jnp.float32, math.log(0.25), math.log(4.0)))
    col_scale = jnp.exp(jax.random.uniform(key_cols, (1, D), jnp.float32, math.log(0.4), math.log(4.0)))
    return (noise * row_scale * col_scale).astype(jnp.bfloat16)


def draw_owner(key, part):
    key = jax.random.fold_in(key, 5)
    sub_keys = jax.random.split(key, N_DEV)
    shuffled = jax.vmap(lambda sub_key: jax.random.permutation(sub_key, K))(sub_keys)
    return (shuffled % N_GROUP).astype(jnp.int32)


def shard_levels(key, extent, shards, least, high):
    level = 1.0
    for dim, parts in shards:
        steps = jax.random.uniform(jax.random.fold_in(jax.random.fold_in(key, 6), dim), (parts,), jnp.float32, least / len(shards), high / len(shards))
        level = level * jnp.repeat(jnp.exp(steps), extent[dim] // parts).reshape((-1,) + (1,) * (len(extent) - 1 - dim))
    return level


def gaussian(stream_key, extent, scale, reach, cuts=(), held_as=jnp.bfloat16):
    result = scale * jax.random.normal(stream_key, extent, jnp.float32)
    if cuts:
        result = result * shard_levels(stream_key, extent, cuts, -0.22, 0.18)
    return jnp.clip(result, -reach, reach).astype(held_as)


def setup_inputs(seed: int = 0) -> dict:
    splits = jax.random.split(jax.random.key(seed), 7)
    tokens = draw_tokens(jax.random.fold_in(splits[6], 71), 0)
    query_grad = gaussian(splits[1], (TOKENS, D), (1.0 / TOKENS ** 0.5), 0.06591797, ((0, 512),))
    gain = jnp.clip(1.0 + 0.18 * jax.random.normal(splits[2], (D,), jnp.float32), 0.1, 1.9)
    master = gaussian(splits[3], (N_DEV, N_GROUP, KG, PART), 1.0, 6.0, ((0, 64), (1, 8)), jnp.float32)
    momentum = gaussian(splits[4], (N_DEV, N_GROUP, KG, PART), 1.0, 6.0, ((0, 64), (1, 8)), jnp.float32)
    owner = draw_owner(jax.random.fold_in(splits[6], 71), 0)
    return {"tokens": tokens, "query_grad": query_grad, "gain": gain, "master": master, "momentum": momentum, "owner": owner}


norm_eps = 1e-05
momentum_rate = 0.9
learn_rate = 0.2

def owner_rank(owner):
    onehot = (owner[..., None] == jnp.arange(N_GROUP, dtype=jnp.int32)).astype(jnp.int32)
    before = jnp.cumsum(onehot, axis=1) - onehot
    return lax.optimization_barrier(jnp.sum(before * onehot, axis=-1)).astype(jnp.int32)

def reference(tokens, query_grad, gain, master, momentum, owner):
    rank_in = owner_rank(owner)
    block_ids = jnp.arange(N_DEV, dtype=jnp.int32)[:, None]
    values = tokens.astype(jnp.float32)
    mean_square = lax.optimization_barrier(jnp.mean(values * values, axis=1, keepdims=True))
    normed = (values * lax.rsqrt(mean_square + norm_eps) * gain[None, :]).astype(jnp.bfloat16)
    gradient = jnp.dot(normed.T, query_grad, preferred_element_type=jnp.float32)
    partitions = gradient.reshape(D, N_DEV, COLS).transpose(1, 0, 2).reshape(N_DEV, K, PART)
    placed = jnp.zeros(master.shape, jnp.float32).at[block_ids, owner, rank_in].set(partitions)
    momentum_new = momentum_rate * momentum + placed
    master_new = master - learn_rate * momentum_new
    gathered = master_new[block_ids, owner, rank_in].reshape(N_DEV, D, COLS)
    params_new = gathered.transpose(1, 0, 2).reshape(D, D).astype(jnp.bfloat16)
    return (master_new, momentum_new, params_new)
```

```python
import functools

import jax
import jax.numpy as jnp
from jax import lax
from jax.experimental import pallas as pl
from jax.experimental.pallas import tpu as pltpu
from jax.sharding import Mesh, PartitionSpec as P

norm_eps = 1e-05
momentum_rate = 0.9
learn_rate = 0.2

PARTS = (("x", 4), ("h", 2), ("y", 8), ("l", 4), ("c", 2))
GROUP = ("x", "h")
DEV = ("y", "l", "c")


def slot_table(owner_row, groups):
    onehot = (owner_row[:, None] == jnp.arange(groups, dtype=jnp.int32)[None, :]).astype(jnp.int32)
    before = jnp.cumsum(onehot, axis=0) - onehot
    return jnp.sum(before * onehot, axis=1)


def spread_x(block):
    return lax.all_to_all(
        jnp.broadcast_to(block[None], (lax.axis_size("x"), *block.shape)), "x", split_axis=0, concat_axis=0, tiled=True
    )


def swap(block, axis):
    return lax.ppermute(block, axis, [(0, 1), (1, 0)])


def finish_kernel(per_group, part_rows, h_ref, source_ref, place_ref, own_ref, other_ref, pulled_ref, master_ref,
                  momentum_ref, master_out, momentum_out, params_out, work_ref):
    a = pl.program_id(0)
    h = h_ref[0]
    columns = params_out.shape[1]
    x = lax.div(a, 2)
    in_own = lax.rem(a, 2) == h
    for p in range(per_group):
        rows = pl.ds(p * part_rows, part_rows)
        held = pulled_ref[place_ref[a * per_group + p]].astype(jnp.float32)

        @pl.when(in_own)
        def _(rows=rows, held=held):
            params_out[rows, :] = (held - learn_rate * own_ref[x, rows, :].astype(jnp.float32)).astype(jnp.bfloat16)

        @pl.when(jnp.logical_not(in_own))
        def _(rows=rows, held=held):
            params_out[rows, :] = (held - learn_rate * other_ref[x, rows, :].astype(jnp.float32)).astype(jnp.bfloat16)

    step = master_ref.shape[1] // columns
    for j in range(per_group):
        k = source_ref[j]
        block = lax.div(k, per_group)
        start = pl.multiple_of(lax.rem(k, per_group) * part_rows + a * step, step)
        bx = lax.div(block, 2)
        mine = own_ref[bx, pl.ds(start, step), :].astype(jnp.float32)
        theirs = other_ref[bx, pl.ds(start, step), :].astype(jnp.float32)
        work_ref[pl.ds(j * step, step), :] = jnp.where(lax.rem(block, 2) == h, mine, theirs)
    for r in range(step):
        grad = work_ref[pl.ds(r, per_group, stride=step), :]
        cols = pl.ds(r * columns, columns)
        momentum_new = momentum_rate * momentum_ref[:, cols] + grad
        momentum_out[:, cols] = momentum_new
        master_out[:, cols] = master_ref[:, cols] - learn_rate * momentum_new


def finish(h, source, place, own, other, pulled, master, momentum):
    nx, rows, columns = own.shape
    part_count, part_rows, _ = pulled.shape
    per_group, part_size = master.shape
    groups = part_count // per_group
    whole = lambda arr: pl.BlockSpec(arr.shape, lambda a, *_: (0,) * arr.ndim)
    served = pl.BlockSpec((per_group, part_size // groups), lambda a, *_: (0, a))
    return pl.pallas_call(
        functools.partial(finish_kernel, per_group, part_rows),
        grid_spec=pltpu.PrefetchScalarGridSpec(
            num_scalar_prefetch=3,
            grid=(groups,),
            in_specs=[whole(own), whole(other), whole(pulled), served, served],
            out_specs=[served, served, pl.BlockSpec((rows, columns), lambda a, *_: (a, 0))],
            scratch_shapes=[pltpu.VMEM((per_group * part_rows // groups, columns), jnp.float32)],
        ),
        out_shape=[
            jax.ShapeDtypeStruct(master.shape, jnp.float32),
            jax.ShapeDtypeStruct(master.shape, jnp.float32),
            jax.ShapeDtypeStruct((groups * rows, columns), jnp.bfloat16),
        ],
        compiler_params=pltpu.CompilerParams(vmem_limit_bytes=24 * 1024 * 1024),
        cost_estimate=pl.CostEstimate(flops=4_000_000, bytes_accessed=8_000_000, transcendentals=0),
        name="finish",
    )(h.reshape(1), source, place, own, other, pulled, master, momentum)


def local(tokens, query_grad, gain, master, momentum, owner):
    nx, nh, ny, nl, nc = (lax.axis_size(name) for name, _ in PARTS)
    groups = nx * nh
    own, width = tokens.shape
    columns = width // (ny * nl * nc)
    rows = width // groups
    part_size = master.shape[-1]
    part_count = owner.shape[1]
    per_group = part_count // groups
    part_rows = part_size // columns
    h = lax.axis_index("h")
    c = lax.axis_index("c")
    me = lax.axis_index(GROUP)

    sent = tokens.reshape(own, nx, nh, rows)
    sent = jnp.concatenate(
        [jnp.where(h == 0, sent[:, :, 0], sent[:, :, 1]), jnp.where(h == 0, sent[:, :, 1], sent[:, :, 0])], axis=0
    )
    sent = sent.transpose(1, 0, 2)
    mine = lax.all_to_all(sent, "x", split_axis=0, concat_axis=0, tiled=True)
    pair = jnp.stack([mine[:, :own], swap(mine[:, own:], "h")])
    left = lax.all_gather(pair, "y", axis=0, tiled=False)

    values = tokens.astype(jnp.float32)
    scale = lax.rsqrt(jnp.mean(values * values, axis=1, keepdims=True) + norm_eps)
    scaled = (query_grad.astype(jnp.float32) * scale).astype(jnp.bfloat16)
    scaled = scaled.reshape(own, ny, nl, nc, columns)
    scaled = jnp.where(c == 0, scaled[:, :, :, ::-1], scaled)
    scaled = scaled.transpose(1, 0, 3, 2, 4).reshape(ny, own, nc * nl * columns)
    part = lax.all_to_all(scaled, "y", split_axis=0, concat_axis=0, tiled=True)
    part_other = swap(part, "h")
    right_own = spread_x(part)
    right_own, part_other = lax.optimization_barrier((right_own, part_other))
    right_other = spread_x(part_other)
    right = jnp.concatenate([right_own, right_other], axis=0)

    before = (master[0, 0] - learn_rate * momentum_rate * momentum[0, 0]).astype(jnp.bfloat16)
    before = before.reshape(per_group, part_rows, columns)
    before, _ = lax.optimization_barrier((before, part_other))
    pair = jnp.stack([before, swap(before, "h")], axis=0)
    pulled = lax.all_gather(pair, "x", axis=0, tiled=False)
    pulled = pulled.reshape(part_count, part_rows, columns)
    owner_row = lax.dynamic_slice_in_dim(owner, lax.axis_index(DEV), 1, 0)[0]
    rank = slot_table(owner_row, groups)
    place = ((owner_row // nh) * nh + jnp.where(owner_row % nh == h, 0, 1)) * per_group + rank
    slots = jnp.arange(per_group, dtype=jnp.int32)
    hit = (owner_row[None, :] == me) & (rank[None, :] == slots[:, None])
    source = jnp.sum(jnp.where(hit, jnp.arange(part_count, dtype=jnp.int32)[None, :], 0), axis=1)

    weight = lax.dynamic_slice_in_dim(gain, me * rows, rows, 0)[:, None]

    def product(half):
        both = right[:, :, :, half * nl * columns : (half + 1) * nl * columns]
        both = both.transpose(1, 0, 2, 3).reshape(-1, nl * columns)
        return weight * lax.dot_general(
            left.reshape(-1, rows), both, (((0,), (0,)), ((), ())), preferred_element_type=jnp.float32
        )

    came = swap(product(0).astype(jnp.bfloat16), "c")
    both = (product(1) + came.astype(jnp.float32)).astype(jnp.bfloat16)
    both = both.reshape(rows, nl, columns).transpose(1, 0, 2)
    got = lax.all_to_all(both, "l", split_axis=0, concat_axis=0, tiled=True)
    summed = jnp.sum(got.astype(jnp.float32), axis=0).astype(jnp.bfloat16)
    summed, pulled, place, source = lax.optimization_barrier((summed, pulled, place, source))

    summed_other = swap(summed, "h")
    full_own = spread_x(summed)
    full_own, summed_other = lax.optimization_barrier((full_own, summed_other))
    full_other = spread_x(summed_other)
    master_new, momentum_new, params_new = finish(
        h, source, place, full_own, full_other, pulled, master[0, 0], momentum[0, 0]
    )
    return (master_new[None, None], momentum_new[None, None], params_new)


def solution(mesh):
    fine = Mesh(mesh.devices.reshape([size for _, size in PARTS]), [name for name, _ in PARTS])
    whole = (*GROUP, *DEV)
    server = P(DEV, GROUP, None, None)
    return jax.shard_map(
        local,
        mesh=fine,
        in_specs=(P(whole, None), P(whole, None), P(), server, server, P()),
        out_specs=(server, server, P(None, DEV)),
        check_vma=False,
    )
```

```python
import functools

import jax
import jax.numpy as jnp
from jax import lax
from jax.experimental import pallas as pl
from jax.experimental.pallas import tpu as pltpu
from jax.sharding import Mesh, PartitionSpec as P

norm_eps = 1e-05
momentum_rate = 0.9
learn_rate = 0.2

PARTS = (("x", 4), ("h", 2), ("y", 8), ("l", 4), ("c", 2))
GROUP = ("x", "h")
DEV = ("y", "l", "c")


def slot_table(owner_row, groups):
    onehot = (owner_row[:, None] == jnp.arange(groups, dtype=jnp.int32)[None, :]).astype(jnp.int32)
    before = jnp.cumsum(onehot, axis=0) - onehot
    return jnp.sum(before * onehot, axis=1)


def spread(block, axis):
    return lax.all_to_all(
        jnp.broadcast_to(block[None], (lax.axis_size(axis), *block.shape)), axis, split_axis=0, concat_axis=0, tiled=True
    )


def swap(block, axis):
    return lax.ppermute(block, axis, [(0, 1), (1, 0)])


def finish_kernel(per_group, part_rows, h_ref, source_ref, place_ref, own_ref, other_ref, pulled_ref, base_master_ref,
                  base_momentum_ref, master_out, momentum_out, params_out, work_ref):
    x = pl.program_id(0)
    h = h_ref[0]
    columns = params_out.shape[1]
    span = per_group * part_rows
    for theirs in range(2):
        block = lax.rem(h + theirs, 2)
        grad_ref = (own_ref, other_ref)[theirs]
        for p in range(per_group):
            held = pulled_ref[place_ref[(x * 2 + block) * per_group + p]].astype(jnp.float32)
            grad = grad_ref[x, p * part_rows : (p + 1) * part_rows, :].astype(jnp.float32)
            rows = pl.ds(pl.multiple_of(block * span + p * part_rows, part_rows), part_rows)
            params_out[rows, :] = (held - learn_rate * grad).astype(jnp.bfloat16)

    step = base_master_ref.shape[1] // columns
    for j in range(per_group):
        k = source_ref[j]
        block = lax.div(k, per_group)
        start = pl.multiple_of(lax.rem(k, per_group) * part_rows + x * step, step)
        bx = lax.div(block, 2)
        mine = own_ref[bx, pl.ds(start, step), :].astype(jnp.float32)
        theirs = other_ref[bx, pl.ds(start, step), :].astype(jnp.float32)
        work_ref[pl.ds(j * step, step), :] = jnp.where(lax.rem(block, 2) == h, mine, theirs)
    for r in range(step):
        grad = work_ref[pl.ds(r, per_group, stride=step), :]
        cols = pl.ds(r * columns, columns)
        momentum_out[:, cols] = base_momentum_ref[:, cols] + grad
        master_out[:, cols] = base_master_ref[:, cols] - learn_rate * grad


def finish(h, source, place, own, other, pulled, master, momentum):
    nx, rows, columns = own.shape
    part_count, part_rows, _ = pulled.shape
    per_group, part_size = master.shape
    groups = part_count // per_group
    whole = lambda arr: pl.BlockSpec(arr.shape, lambda a, *_: (0,) * arr.ndim)
    served = pl.BlockSpec((per_group, part_size // nx), lambda a, *_: (0, a))
    return pl.pallas_call(
        functools.partial(finish_kernel, per_group, part_rows),
        grid_spec=pltpu.PrefetchScalarGridSpec(
            num_scalar_prefetch=3,
            grid=(nx,),
            in_specs=[whole(own), whole(other), whole(pulled), served, served],
            out_specs=[served, served, pl.BlockSpec((groups // nx * rows, columns), lambda a, *_: (a, 0))],
            scratch_shapes=[pltpu.VMEM((per_group * part_rows // nx, columns), jnp.float32)],
        ),
        out_shape=[
            jax.ShapeDtypeStruct(master.shape, jnp.float32),
            jax.ShapeDtypeStruct(master.shape, jnp.float32),
            jax.ShapeDtypeStruct((groups * rows, columns), jnp.bfloat16),
        ],
        compiler_params=pltpu.CompilerParams(vmem_limit_bytes=24 * 1024 * 1024),
        cost_estimate=pl.CostEstimate(flops=4_000_000, bytes_accessed=8_000_000, transcendentals=0),
        name="finish",
    )(h.reshape(1), source, place, own, other, pulled, master, momentum)


def local(tokens, query_grad, gain, master, momentum, owner):
    nx, nh, ny, nl, nc = (lax.axis_size(name) for name, _ in PARTS)
    groups = nx * nh
    own, width = tokens.shape
    columns = width // (ny * nl * nc)
    rows = width // groups
    part_size = master.shape[-1]
    part_count = owner.shape[1]
    per_group = part_count // groups
    part_rows = part_size // columns
    h = lax.axis_index("h")
    c = lax.axis_index("c")
    me = lax.axis_index(GROUP)

    sent = tokens.reshape(own, nx, nc, rows)
    sent = jnp.concatenate(
        [jnp.where(c == 0, sent[:, :, 0], sent[:, :, 1]), jnp.where(c == 0, sent[:, :, 1], sent[:, :, 0])], axis=0
    )
    sent = sent.transpose(1, 0, 2)
    mine = lax.all_to_all(sent, "x", split_axis=0, concat_axis=0, tiled=True)
    pair = jnp.stack([mine[:, :own], swap(mine[:, own:], "c")])
    left = lax.all_gather(pair, "y", axis=0, tiled=False)

    values = tokens.astype(jnp.float32)
    scale = lax.rsqrt(jnp.mean(values * values, axis=1, keepdims=True) + norm_eps)
    scaled = (query_grad.astype(jnp.float32) * scale).astype(jnp.bfloat16)
    scaled = scaled.reshape(own, ny, nl, nc, columns)
    scaled = jnp.where(c == 0, scaled, scaled[:, :, :, ::-1])
    scaled = scaled.transpose(1, 0, 3, 2, 4).reshape(ny, own, nc * nl * columns)

    def past(master, momentum):
        block = (master - learn_rate * momentum_rate * momentum).astype(jnp.bfloat16)
        return block.reshape(per_group, part_rows, columns)

    scaled, pair = lax.optimization_barrier((scaled, pair))
    part = lax.all_to_all(scaled, "y", split_axis=0, concat_axis=0, tiled=True)
    before_other, part = lax.optimization_barrier((past(master[0, 0], momentum[0, 0]), part))
    before_other = swap(before_other, "h")
    right_own = spread(part, "x")
    right_own, before_other = lax.optimization_barrier((right_own, before_other))
    right_other = swap(right_own, "c")
    half = nl * columns
    halves = [
        jnp.concatenate([right_own[..., :half], right_other[..., half:]]),
        jnp.concatenate([right_own[..., half:], right_other[..., :half]]),
    ]

    owner_row = lax.dynamic_slice_in_dim(owner, lax.axis_index(DEV), 1, 0)[0]
    rank = slot_table(owner_row, groups)
    place = (jnp.where(owner_row % nh == h, 0, nx) + owner_row // nh) * per_group + rank
    slots = jnp.arange(per_group, dtype=jnp.int32)
    hit = (owner_row[None, :] == me) & (rank[None, :] == slots[:, None])
    source = jnp.sum(jnp.where(hit, jnp.arange(part_count, dtype=jnp.int32)[None, :], 0), axis=1)

    weight = lax.dynamic_slice_in_dim(gain, (lax.axis_index("x") * nc + c) * rows, rows, 0)[:, None]

    def product(right):
        out = lax.dot_general(
            left.reshape(-1, rows),
            right.transpose(1, 0, 2, 3).reshape(-1, half),
            (((0,), (0,)), ((), ())),
            preferred_element_type=jnp.float32,
        )
        return (weight * out).astype(jnp.bfloat16)

    came = swap(product(halves[1]), "c")
    keep = product(halves[0])
    both = jnp.concatenate([block.reshape(rows, nl, columns).transpose(1, 0, 2) for block in (keep, came)])
    both = both.reshape(nh * nl * rows, columns)
    summed = lax.psum_scatter(both, ("h", "l"), scatter_dimension=0, tiled=True)

    base_master, base_momentum, _ = lax.optimization_barrier((master[0, 0], momentum[0, 0], came))
    before_own = spread(past(base_master, base_momentum), "x")
    before_own, before_other = lax.optimization_barrier((before_own, before_other))
    before_other = spread(before_other, "x")
    pulled = jnp.concatenate([before_own, before_other]).reshape(part_count, part_rows, columns)
    base_master = base_master - learn_rate * momentum_rate * base_momentum
    base_momentum = momentum_rate * base_momentum
    summed, pulled, place, source, base_master, base_momentum = lax.optimization_barrier(
        (summed, pulled, place, source, base_master, base_momentum)
    )

    full_own = lax.all_gather(summed, "x", axis=0, tiled=False)
    full_other = spread(swap(summed, "h"), "x")
    master_new, momentum_new, params_new = finish(
        lax.rem(h + c, nh), source, place, full_own, full_other, pulled, base_master, base_momentum
    )
    return (master_new[None, None], momentum_new[None, None], params_new)


def solution(mesh):
    fine = Mesh(mesh.devices.reshape([size for _, size in PARTS]), [name for name, _ in PARTS])
    whole = (*GROUP, *DEV)
    server = P(DEV, GROUP, None, None)
    return jax.shard_map(
        local,
        mesh=fine,
        in_specs=(P(whole, None), P(whole, None), P(), server, server, P()),
        out_specs=(server, server, P(None, DEV)),
        check_vma=False,
    )
```

```python
import functools

import jax
import jax.numpy as jnp
from jax import lax
from jax.experimental import pallas as pl
from jax.experimental.pallas import tpu as pltpu
from jax.sharding import Mesh, PartitionSpec as P

norm_eps = 1e-05
momentum_rate = 0.9
learn_rate = 0.2

PARTS = (("x", 4), ("h", 2), ("y", 8), ("l", 4), ("c", 2))
GROUP = ("x", "h")
DEV = ("y", "l", "c")


def slot_table(owner_row, groups):
    onehot = (owner_row[:, None] == jnp.arange(groups, dtype=jnp.int32)[None, :]).astype(jnp.int32)
    before = jnp.cumsum(onehot, axis=0) - onehot
    return jnp.sum(before * onehot, axis=1)


def spread(block, axis):
    return lax.all_to_all(
        jnp.broadcast_to(block[None], (lax.axis_size(axis), *block.shape)), axis, split_axis=0, concat_axis=0, tiled=True
    )


def swap(block, axis):
    return lax.ppermute(block, axis, [(0, 1), (1, 0)])


def finish_kernel(per_group, part_rows, h_ref, source_ref, place_ref, own_ref, other_ref, pulled_ref, base_master_ref,
                  base_momentum_ref, master_out, momentum_out, params_out, work_ref):
    x = pl.program_id(0)
    h = h_ref[0]
    columns = params_out.shape[1]
    span = per_group * part_rows
    for theirs in range(2):
        block = lax.rem(h + theirs, 2)
        grad_ref = (own_ref, other_ref)[theirs]
        for p in range(per_group):
            held = pulled_ref[place_ref[(x * 2 + block) * per_group + p]].astype(jnp.float32)
            grad = grad_ref[x, p * part_rows : (p + 1) * part_rows, :].astype(jnp.float32)
            rows = pl.ds(pl.multiple_of(block * span + p * part_rows, part_rows), part_rows)
            params_out[rows, :] = (held - learn_rate * grad).astype(jnp.bfloat16)

    step = base_master_ref.shape[1] // columns
    for j in range(per_group):
        k = source_ref[j]
        block = lax.div(k, per_group)
        start = pl.multiple_of(lax.rem(k, per_group) * part_rows + x * step, step)
        bx = lax.div(block, 2)
        mine = own_ref[bx, pl.ds(start, step), :].astype(jnp.float32)
        theirs = other_ref[bx, pl.ds(start, step), :].astype(jnp.float32)
        work_ref[pl.ds(j * step, step), :] = jnp.where(lax.rem(block, 2) == h, mine, theirs)
    for r in range(step):
        grad = work_ref[pl.ds(r, per_group, stride=step), :]
        cols = pl.ds(r * columns, columns)
        momentum_out[:, cols] = base_momentum_ref[:, cols] + grad
        master_out[:, cols] = base_master_ref[:, cols] - learn_rate * grad


def finish(h, source, place, own, other, pulled, master, momentum):
    nx, rows, columns = own.shape
    part_count, part_rows, _ = pulled.shape
    per_group, part_size = master.shape
    groups = part_count // per_group
    whole = lambda arr: pl.BlockSpec(arr.shape, lambda a, *_: (0,) * arr.ndim)
    served = pl.BlockSpec((per_group, part_size // nx), lambda a, *_: (0, a))
    return pl.pallas_call(
        functools.partial(finish_kernel, per_group, part_rows),
        grid_spec=pltpu.PrefetchScalarGridSpec(
            num_scalar_prefetch=3,
            grid=(nx,),
            in_specs=[whole(own), whole(other), whole(pulled), served, served],
            out_specs=[served, served, pl.BlockSpec((groups // nx * rows, columns), lambda a, *_: (a, 0))],
            scratch_shapes=[pltpu.VMEM((per_group * part_rows // nx, columns), jnp.float32)],
        ),
        out_shape=[
            jax.ShapeDtypeStruct(master.shape, jnp.float32),
            jax.ShapeDtypeStruct(master.shape, jnp.float32),
            jax.ShapeDtypeStruct((groups * rows, columns), jnp.bfloat16),
        ],
        compiler_params=pltpu.CompilerParams(vmem_limit_bytes=24 * 1024 * 1024),
        cost_estimate=pl.CostEstimate(flops=4_000_000, bytes_accessed=8_000_000, transcendentals=0),
        name="finish",
    )(h.reshape(1), source, place, own, other, pulled, master, momentum)


def local(tokens, query_grad, gain, master, momentum, owner):
    nx, nh, ny, nl, nc = (lax.axis_size(name) for name, _ in PARTS)
    groups = nx * nh
    own, width = tokens.shape
    columns = width // (ny * nl * nc)
    rows = width // groups
    part_size = master.shape[-1]
    part_count = owner.shape[1]
    per_group = part_count // groups
    part_rows = part_size // columns
    h = lax.axis_index("h")
    c = lax.axis_index("c")
    me = lax.axis_index(GROUP)

    sent = tokens.reshape(own, nx * nc, rows).transpose(1, 0, 2)
    mine = lax.all_to_all(sent, ("x", "c"), split_axis=0, concat_axis=0, tiled=True)
    left = lax.all_gather(mine, "y", axis=0, tiled=False)

    values = tokens.astype(jnp.float32)
    scale = lax.rsqrt(jnp.mean(values * values, axis=1, keepdims=True) + norm_eps)
    scaled = (query_grad.astype(jnp.float32) * scale).astype(jnp.bfloat16)
    scaled = scaled.reshape(own, ny, nl, nc, columns)
    scaled = jnp.where(c == 0, scaled, scaled[:, :, :, ::-1])
    scaled = scaled.transpose(1, 0, 3, 2, 4).reshape(ny, own, nc * nl * columns)

    def past(master, momentum):
        block = (master - learn_rate * momentum_rate * momentum).astype(jnp.bfloat16)
        return block.reshape(per_group, part_rows, columns)

    scaled, mine = lax.optimization_barrier((scaled, mine))
    part = lax.all_to_all(scaled, "y", split_axis=0, concat_axis=0, tiled=True)
    before_other, part = lax.optimization_barrier((past(master[0, 0], momentum[0, 0]), part))
    before_other = swap(before_other, "h")
    right_own = spread(part, "x")
    right_own, before_other = lax.optimization_barrier((right_own, before_other))
    right_other = swap(right_own, "c")
    half = nl * columns

    def by_core(ours, theirs):
        return jnp.stack([jnp.where(c == 0, ours, theirs), jnp.where(c == 0, theirs, ours)], axis=1)

    halves = [
        by_core(right_own[..., :half], right_other[..., half:]),
        by_core(right_own[..., half:], right_other[..., :half]),
    ]

    owner_row = lax.dynamic_slice_in_dim(owner, lax.axis_index(DEV), 1, 0)[0]
    rank = slot_table(owner_row, groups)
    place = (jnp.where(owner_row % nh == h, 0, nx) + owner_row // nh) * per_group + rank
    slots = jnp.arange(per_group, dtype=jnp.int32)
    hit = (owner_row[None, :] == me) & (rank[None, :] == slots[:, None])
    source = jnp.sum(jnp.where(hit, jnp.arange(part_count, dtype=jnp.int32)[None, :], 0), axis=1)

    weight = lax.dynamic_slice_in_dim(gain, (lax.axis_index("x") * nc + c) * rows, rows, 0)[:, None]

    def product(right):
        out = lax.dot_general(
            left.reshape(-1, rows),
            right.transpose(2, 0, 1, 3, 4).reshape(-1, half),
            (((0,), (0,)), ((), ())),
            preferred_element_type=jnp.float32,
        )
        return (weight * out).astype(jnp.bfloat16)

    came = swap(product(halves[1]), "c")
    keep = product(halves[0])
    both = jnp.concatenate([block.reshape(rows, nl, columns).transpose(1, 0, 2) for block in (keep, came)])
    both = both.reshape(nh * nl * rows, columns)
    summed = lax.psum_scatter(both, ("h", "l"), scatter_dimension=0, tiled=True)

    base_master, base_momentum, _ = lax.optimization_barrier((master[0, 0], momentum[0, 0], came))
    before_own = spread(past(base_master, base_momentum), "x")
    before_own, before_other = lax.optimization_barrier((before_own, before_other))
    before_other = spread(before_other, "x")
    pulled = jnp.concatenate([before_own, before_other]).reshape(part_count, part_rows, columns)
    base_master = base_master - learn_rate * momentum_rate * base_momentum
    base_momentum = momentum_rate * base_momentum
    summed, pulled, place, source, base_master, base_momentum = lax.optimization_barrier(
        (summed, pulled, place, source, base_master, base_momentum)
    )

    full_own = lax.all_gather(summed, "x", axis=0, tiled=False)
    full_other = spread(swap(summed, "h"), "x")
    master_new, momentum_new, params_new = finish(
        lax.rem(h + c, nh), source, place, full_own, full_other, pulled, base_master, base_momentum
    )
    return (master_new[None, None], momentum_new[None, None], params_new)


def solution(mesh):
    fine = Mesh(mesh.devices.reshape([size for _, size in PARTS]), [name for name, _ in PARTS])
    whole = (*GROUP, *DEV)
    server = P(DEV, GROUP, None, None)
    return jax.shard_map(
        local,
        mesh=fine,
        in_specs=(P(whole, None), P(whole, None), P(), server, server, P()),
        out_specs=(server, server, P(None, DEV)),
        check_vma=False,
    )
```

```python
import functools

import jax
import jax.numpy as jnp
from jax import lax
from jax.experimental import pallas as pl
from jax.experimental.pallas import tpu as pltpu
from jax.sharding import Mesh, PartitionSpec as P

norm_eps = 1e-05
momentum_rate = 0.9
learn_rate = 0.2

PARTS = (("x", 4), ("h", 2), ("y", 8), ("l", 4), ("c", 2))
GROUP = ("x", "h")
DEV = ("y", "l", "c")


def slot_table(owner_row, groups):
    onehot = (owner_row[:, None] == jnp.arange(groups, dtype=jnp.int32)[None, :]).astype(jnp.int32)
    before = jnp.cumsum(onehot, axis=0) - onehot
    return jnp.sum(before * onehot, axis=1)


def spread(block, axis):
    return lax.all_to_all(
        jnp.broadcast_to(block[None], (lax.axis_size(axis), *block.shape)), axis, split_axis=0, concat_axis=0, tiled=True
    )


def swap(block, axis):
    return lax.ppermute(block, axis, [(0, 1), (1, 0)])


def finish_kernel(per_group, part_rows, h_ref, source_ref, place_ref, own_ref, other_ref, pulled_ref, base_master_ref,
                  base_momentum_ref, master_out, momentum_out, params_out, work_ref):
    x = pl.program_id(0)
    h = h_ref[0]
    columns = params_out.shape[1]
    span = per_group * part_rows
    for theirs in range(2):
        block = lax.rem(h + theirs, 2)
        grad_ref = (own_ref, other_ref)[theirs]
        for p in range(per_group):
            held = pulled_ref[place_ref[(x * 2 + block) * per_group + p]].astype(jnp.float32)
            grad = grad_ref[x, p * part_rows : (p + 1) * part_rows, :].astype(jnp.float32)
            rows = pl.ds(pl.multiple_of(block * span + p * part_rows, part_rows), part_rows)
            params_out[rows, :] = (held - learn_rate * grad).astype(jnp.bfloat16)

    step = base_master_ref.shape[1] // columns
    for j in range(per_group):
        k = source_ref[j]
        block = lax.div(k, per_group)
        start = pl.multiple_of(lax.rem(k, per_group) * part_rows + x * step, step)
        bx = lax.div(block, 2)
        mine = own_ref[bx, pl.ds(start, step), :].astype(jnp.float32)
        theirs = other_ref[bx, pl.ds(start, step), :].astype(jnp.float32)
        work_ref[pl.ds(j * step, step), :] = jnp.where(lax.rem(block, 2) == h, mine, theirs)
    for r in range(step):
        grad = work_ref[pl.ds(r, per_group, stride=step), :]
        cols = pl.ds(r * columns, columns)
        momentum_out[:, cols] = base_momentum_ref[:, cols] + grad
        master_out[:, cols] = base_master_ref[:, cols] - learn_rate * grad


def finish(h, source, place, own, other, pulled, master, momentum):
    nx, rows, columns = own.shape
    part_count, part_rows, _ = pulled.shape
    per_group, part_size = master.shape
    groups = part_count // per_group
    whole = lambda arr: pl.BlockSpec(arr.shape, lambda a, *_: (0,) * arr.ndim)
    served = pl.BlockSpec((per_group, part_size // nx), lambda a, *_: (0, a))
    return pl.pallas_call(
        functools.partial(finish_kernel, per_group, part_rows),
        grid_spec=pltpu.PrefetchScalarGridSpec(
            num_scalar_prefetch=3,
            grid=(nx,),
            in_specs=[whole(own), whole(other), whole(pulled), served, served],
            out_specs=[served, served, pl.BlockSpec((groups // nx * rows, columns), lambda a, *_: (a, 0))],
            scratch_shapes=[pltpu.VMEM((per_group * part_rows // nx, columns), jnp.float32)],
        ),
        out_shape=[
            jax.ShapeDtypeStruct(master.shape, jnp.float32),
            jax.ShapeDtypeStruct(master.shape, jnp.float32),
            jax.ShapeDtypeStruct((groups * rows, columns), jnp.bfloat16),
        ],
        compiler_params=pltpu.CompilerParams(vmem_limit_bytes=24 * 1024 * 1024),
        cost_estimate=pl.CostEstimate(flops=4_000_000, bytes_accessed=8_000_000, transcendentals=0),
        name="finish",
    )(h.reshape(1), source, place, own, other, pulled, master, momentum)


def local(tokens, query_grad, gain, master, momentum, owner):
    nx, nh, ny, nl, nc = (lax.axis_size(name) for name, _ in PARTS)
    groups = nx * nh
    own, width = tokens.shape
    columns = width // (ny * nl * nc)
    rows = width // groups
    part_size = master.shape[-1]
    part_count = owner.shape[1]
    per_group = part_count // groups
    part_rows = part_size // columns
    h = lax.axis_index("h")
    c = lax.axis_index("c")
    me = lax.axis_index(GROUP)

    sent = tokens.reshape(own, nx * nc, rows).transpose(1, 0, 2)
    mine = lax.all_to_all(sent, ("x", "c"), split_axis=0, concat_axis=0, tiled=True)
    left = lax.all_gather(mine, "y", axis=0, tiled=False)

    values = tokens.astype(jnp.float32)
    scale = lax.rsqrt(jnp.mean(values * values, axis=1, keepdims=True) + norm_eps)
    scaled = (query_grad.astype(jnp.float32) * scale).astype(jnp.bfloat16)
    scaled = scaled.reshape(own, ny, nl, nc, columns)
    scaled = jnp.where(c == 0, scaled, scaled[:, :, :, ::-1])
    scaled = scaled.transpose(1, 0, 3, 2, 4).reshape(ny, own, nc * nl * columns)

    def past(master, momentum):
        block = (master - learn_rate * momentum_rate * momentum).astype(jnp.bfloat16)
        return block.reshape(per_group, part_rows, columns)

    scaled, mine = lax.optimization_barrier((scaled, mine))
    part = lax.all_to_all(scaled, "y", split_axis=0, concat_axis=0, tiled=True)
    before_other, part = lax.optimization_barrier((past(master[0, 0], momentum[0, 0]), part))
    before_other = swap(before_other, "h")
    right_own = spread(part, "x")
    right_own, before_other = lax.optimization_barrier((right_own, before_other))
    right_other = swap(right_own, "c")
    half = nl * columns

    def by_core(ours, theirs):
        return jnp.stack([jnp.where(c == 0, ours, theirs), jnp.where(c == 0, theirs, ours)], axis=1)

    halves = [
        by_core(right_own[..., :half], right_other[..., half:]),
        by_core(right_own[..., half:], right_other[..., :half]),
    ]

    owner_row = lax.dynamic_slice_in_dim(owner, lax.axis_index(DEV), 1, 0)[0]
    rank = slot_table(owner_row, groups)
    place = (owner_row // nh * nh + jnp.where(owner_row % nh == h, 0, 1)) * per_group + rank
    slots = jnp.arange(per_group, dtype=jnp.int32)
    hit = (owner_row[None, :] == me) & (rank[None, :] == slots[:, None])
    source = jnp.sum(jnp.where(hit, jnp.arange(part_count, dtype=jnp.int32)[None, :], 0), axis=1)

    weight = lax.dynamic_slice_in_dim(gain, (lax.axis_index("x") * nc + c) * rows, rows, 0)[None]

    def product(right):
        out = lax.dot_general(
            right.transpose(2, 0, 1, 3, 4).reshape(-1, half),
            left.reshape(-1, rows),
            (((0,), (0,)), ((), ())),
            preferred_element_type=jnp.float32,
        )
        return (weight * out).astype(jnp.bfloat16)

    came = swap(product(halves[1]), "c")
    keep = product(halves[0])
    both = jnp.concatenate([keep, came])
    summed = lax.psum_scatter(both, ("h", "l"), scatter_dimension=0, tiled=True).T

    base_master, base_momentum, _ = lax.optimization_barrier((master[0, 0], momentum[0, 0], came))
    both_h = jnp.stack([past(base_master, base_momentum), before_other])
    pulled = spread(both_h, "x").reshape(part_count, part_rows, columns)
    base_master = base_master - learn_rate * momentum_rate * base_momentum
    base_momentum = momentum_rate * base_momentum
    summed, pulled, place, source, base_master, base_momentum = lax.optimization_barrier(
        (summed, pulled, place, source, base_master, base_momentum)
    )

    full_own = lax.all_gather(summed, "x", axis=0, tiled=False)
    full_other = spread(swap(summed, "h"), "x")
    master_new, momentum_new, params_new = finish(
        lax.rem(h + c, nh), source, place, full_own, full_other, pulled, base_master, base_momentum
    )
    return (master_new[None, None], momentum_new[None, None], params_new)


def solution(mesh):
    fine = Mesh(mesh.devices.reshape([size for _, size in PARTS]), [name for name, _ in PARTS])
    whole = (*GROUP, *DEV)
    server = P(DEV, GROUP, None, None)
    return jax.shard_map(
        local,
        mesh=fine,
        in_specs=(P(whole, None), P(whole, None), P(), server, server, P()),
        out_specs=(server, server, P(None, DEV)),
        check_vma=False,
    )
```

```python
import functools

import jax
import jax.numpy as jnp
from jax import lax
from jax.experimental import pallas as pl
from jax.experimental.pallas import tpu as pltpu
from jax.sharding import Mesh, PartitionSpec as P

norm_eps = 1e-05
momentum_rate = 0.9
learn_rate = 0.2

PARTS = (("x", 4), ("h", 2), ("y", 8), ("l", 4), ("c", 2))
GROUP = ("x", "h")
DEV = ("y", "l", "c")


def slot_table(owner_row, groups):
    onehot = (owner_row[:, None] == jnp.arange(groups, dtype=jnp.int32)[None, :]).astype(jnp.int32)
    before = jnp.cumsum(onehot, axis=0) - onehot
    return jnp.sum(before * onehot, axis=1)


def spread(block, axis):
    return lax.all_to_all(
        jnp.broadcast_to(block[None], (lax.axis_size(axis), *block.shape)), axis, split_axis=0, concat_axis=0, tiled=True
    )


def swap(block, axis):
    return lax.ppermute(block, axis, [(0, 1), (1, 0)])


def finish_kernel(per_group, part_rows, h_ref, source_ref, place_ref, own_ref, other_ref, pulled_ref, base_master_ref,
                  base_momentum_ref, master_out, momentum_out, params_out, work_ref):
    x = pl.program_id(0)
    h = h_ref[0]
    columns = params_out.shape[1]
    span = per_group * part_rows
    for theirs in range(2):
        block = lax.rem(h + theirs, 2)
        grad_ref = (own_ref, other_ref)[theirs]
        for p in range(per_group):
            held = pulled_ref[place_ref[(x * 2 + block) * per_group + p]].astype(jnp.float32)
            grad = grad_ref[x, p * part_rows : (p + 1) * part_rows, :].astype(jnp.float32)
            rows = pl.ds(pl.multiple_of(block * span + p * part_rows, part_rows), part_rows)
            params_out[rows, :] = (held - learn_rate * grad).astype(jnp.bfloat16)

    step = base_master_ref.shape[1] // columns
    for j in range(per_group):
        k = source_ref[j]
        block = lax.div(k, per_group)
        start = pl.multiple_of(lax.rem(k, per_group) * part_rows + x * step, step)
        bx = lax.div(block, 2)
        mine = own_ref[bx, pl.ds(start, step), :].astype(jnp.float32)
        theirs = other_ref[bx, pl.ds(start, step), :].astype(jnp.float32)
        work_ref[pl.ds(j * step, step), :] = jnp.where(lax.rem(block, 2) == h, mine, theirs)
    for r in range(step):
        grad = work_ref[pl.ds(r, per_group, stride=step), :]
        cols = pl.ds(r * columns, columns)
        momentum_out[:, cols] = base_momentum_ref[:, cols] + grad
        master_out[:, cols] = base_master_ref[:, cols] - learn_rate * grad


def finish(h, source, place, own, other, pulled, master, momentum):
    nx, rows, columns = own.shape
    part_count, part_rows, _ = pulled.shape
    per_group, part_size = master.shape
    groups = part_count // per_group
    whole = lambda arr: pl.BlockSpec(arr.shape, lambda a, *_: (0,) * arr.ndim)
    served = pl.BlockSpec((per_group, part_size // nx), lambda a, *_: (0, a))
    return pl.pallas_call(
        functools.partial(finish_kernel, per_group, part_rows),
        grid_spec=pltpu.PrefetchScalarGridSpec(
            num_scalar_prefetch=3,
            grid=(nx,),
            in_specs=[whole(own), whole(other), whole(pulled), served, served],
            out_specs=[served, served, pl.BlockSpec((groups // nx * rows, columns), lambda a, *_: (a, 0))],
            scratch_shapes=[pltpu.VMEM((per_group * part_rows // nx, columns), jnp.float32)],
        ),
        out_shape=[
            jax.ShapeDtypeStruct(master.shape, jnp.float32),
            jax.ShapeDtypeStruct(master.shape, jnp.float32),
            jax.ShapeDtypeStruct((groups * rows, columns), jnp.bfloat16),
        ],
        compiler_params=pltpu.CompilerParams(vmem_limit_bytes=50 * 1024 * 1024),
        cost_estimate=pl.CostEstimate(flops=4_000_000, bytes_accessed=8_000_000, transcendentals=0),
        name="finish",
    )(h.reshape(1), source, place, own, other, pulled, master, momentum)


def local(tokens, query_grad, gain, master, momentum, owner):
    nx, nh, ny, nl, nc = (lax.axis_size(name) for name, _ in PARTS)
    groups = nx * nh
    own, width = tokens.shape
    columns = width // (ny * nl * nc)
    rows = width // groups
    part_size = master.shape[-1]
    part_count = owner.shape[1]
    per_group = part_count // groups
    part_rows = part_size // columns
    h = lax.axis_index("h")
    c = lax.axis_index("c")
    me = lax.axis_index(GROUP)

    sent = tokens.reshape(own, nx * nc, rows).transpose(1, 0, 2)
    mine = lax.all_to_all(sent, ("x", "c"), split_axis=0, concat_axis=0, tiled=True)
    left = lax.all_gather(mine, "y", axis=0, tiled=False)

    values = tokens.astype(jnp.float32)
    scale = lax.rsqrt(jnp.mean(values * values, axis=1, keepdims=True) + norm_eps)
    scaled = (query_grad.astype(jnp.float32) * scale).astype(jnp.bfloat16)
    scaled = scaled.reshape(own, ny, nl, nc, columns)
    scaled = jnp.where(c == 0, scaled, scaled[:, :, :, ::-1])
    scaled = scaled.transpose(1, 0, 3, 2, 4).reshape(ny, own, nc * nl * columns)

    def past(master, momentum):
        block = (master - learn_rate * momentum_rate * momentum).astype(jnp.bfloat16)
        return block.reshape(per_group, part_rows, columns)

    scaled, mine = lax.optimization_barrier((scaled, mine))
    part = lax.all_to_all(scaled, "y", split_axis=0, concat_axis=0, tiled=True)
    before_other, part = lax.optimization_barrier((past(master[0, 0], momentum[0, 0]), part))
    before_other = swap(before_other, "h")
    right_own = spread(part, "x")
    right_own, before_other = lax.optimization_barrier((right_own, before_other))
    right_other = swap(right_own, "c")
    half = nl * columns

    def by_core(ours, theirs):
        return jnp.stack([jnp.where(c == 0, ours, theirs), jnp.where(c == 0, theirs, ours)], axis=1)

    halves = [
        by_core(right_own[..., :half], right_other[..., half:]),
        by_core(right_own[..., half:], right_other[..., :half]),
    ]

    owner_row = lax.dynamic_slice_in_dim(owner, lax.axis_index(DEV), 1, 0)[0]
    rank = slot_table(owner_row, groups)
    place = (owner_row // nh * nh + jnp.where(owner_row % nh == h, 0, 1)) * per_group + rank
    slots = jnp.arange(per_group, dtype=jnp.int32)
    hit = (owner_row[None, :] == me) & (rank[None, :] == slots[:, None])
    source = jnp.sum(jnp.where(hit, jnp.arange(part_count, dtype=jnp.int32)[None, :], 0), axis=1)

    weight = lax.dynamic_slice_in_dim(gain, (lax.axis_index("x") * nc + c) * rows, rows, 0)[None]

    def product(right):
        out = lax.dot_general(
            right.transpose(2, 0, 1, 3, 4).reshape(-1, half),
            left.reshape(-1, rows),
            (((0,), (0,)), ((), ())),
            preferred_element_type=jnp.float32,
        )
        return (weight * out).astype(jnp.bfloat16)

    came = swap(product(halves[1]), "c")
    keep = product(halves[0])
    both = jnp.concatenate([keep, came])
    summed = lax.psum_scatter(both, ("h", "l"), scatter_dimension=0, tiled=True).T

    base_master, base_momentum, _ = lax.optimization_barrier((master[0, 0], momentum[0, 0], came))
    both_h = jnp.stack([past(base_master, base_momentum), before_other])
    pulled = spread(both_h, "x").reshape(part_count, part_rows, columns)
    base_master = base_master - learn_rate * momentum_rate * base_momentum
    base_momentum = momentum_rate * base_momentum
    summed, pulled, place, source, base_master, base_momentum = lax.optimization_barrier(
        (summed, pulled, place, source, base_master, base_momentum)
    )

    full_own = lax.all_gather(summed, "x", axis=0, tiled=False)
    full_other = spread(swap(summed, "h"), "x")
    master_new, momentum_new, params_new = finish(
        lax.rem(h + c, nh), source, place, full_own, full_other, pulled, base_master, base_momentum
    )
    return (master_new[None, None], momentum_new[None, None], params_new)


def solution(mesh):
    fine = Mesh(mesh.devices.reshape([size for _, size in PARTS]), [name for name, _ in PARTS])
    whole = (*GROUP, *DEV)
    server = P(DEV, GROUP, None, None)
    return jax.shard_map(
        local,
        mesh=fine,
        in_specs=(P(whole, None), P(whole, None), P(), server, server, P()),
        out_specs=(server, server, P(None, DEV)),
        check_vma=False,
    )
```
